32 devices in a mesh: groups: 2 (over x), ctx: 8 (over z, y), heads: 2 (over core).
Axes of the slice: x: 2, y: 2, z: 4, core: 2. Of those that a mesh axis runs over, the one named last changes fastest.
Arguments:
- activations: bfloat16 [8192, 4096], P(('groups', 'ctx')), parts along dimension 0, may hold values from -6 to 6
- queries: bfloat16 [8192, 2048], P(('groups', 'ctx'), 'heads'), parts along dimension 0, may hold values from -6 to 6
- key_rows: bfloat16 [8192, 2048], P(('groups', 'ctx'), 'heads'), parts along dimension 0, may hold values from -6 to 6
- value_rows: bfloat16 [8192, 2048], P(('groups', 'ctx'), 'heads'), parts along dimension 0, may hold values from -6 to 6
- out_grad: bfloat16 [8192, 2048], P(('groups', 'ctx'), 'heads'), parts along dimension 0, may hold values from -6 to 6
- norm_gain: float32 [2048], P('heads'), may hold values from 0.1 to 1.9
Outputs:
- query_grad: bfloat16 [8192, 2048], P(('groups', 'ctx'), 'heads'), parts along dimension 0
- key_grad: bfloat16 [8192, 2048], P(('groups', 'ctx'), 'heads'), parts along dimension 0
- weight_grad: float32 [8192, 2048], P(('groups', 'ctx'), 'heads'), parts along dimension 0
The draws below stay inside these ranges and needn't reach their ends.
There are 2 independent parts, one for each index of `groups`. The reference program is written for one: setup_inputs(seed, part) draws one part's arguments, and reference() takes and returns one part's arrays. A program takes and returns all parts, laid end to end along the dimension named above; an argument that names none is the same for every part. Nothing has to cross between parts.
All inputs are finite; a program needn't handle non-finite values.
Results may differ from the reference program's by a relative error of at most 0.015.
Values may be sent and summed in bfloat16 or wider, within the bound.
A program may use at most 128 MiB of HBM per device.

```python
import jax
import jax.numpy as jnp
from jax import lax

D = 4096
HEAD_DIM = 128
HEADS = 16
TOK_DEV = 512
TOKENS = 4096
N_CTX = 8


def strengthened(entries, rng, source, target, blocks, factor):
    owner, partner = [(jnp.arange(entries.shape[position]) // (entries.shape[position] // blocks)).reshape([-1 if axis == position else 1 for axis in range(entries.ndim)]) for position in (source, target)]
    chosen = jax.random.permutation(rng, blocks)[partner]
    strong = (owner == chosen) | (owner == (partner + blocks // 2) % blocks)
    return jnp.where(strong, factor * entries, entries)


def level_of(rng, extent, split, smallest, top_value):
    factor_of = 1.0
    for axis_at, blocks in split:
        steps = jax.random.uniform(jax.random.fold_in(jax.random.fold_in(rng, 6), axis_at), (blocks,), jnp.float32, smallest / len(split), top_value / len(split))
        factor_of = factor_of * jnp.repeat(jnp.exp(steps), extent[axis_at] // blocks).reshape((-1,) + (1,) * (len(extent) - 1 - axis_at))
    return factor_of


def noise(rng, shape, spread, most, shards=(), dtype=jnp.bfloat16):
    values = spread * jax.random.normal(rng, shape, jnp.float32)
    if shards:
        values = values * level_of(rng, shape, shards, -0.22, 0.18)
    return jnp.clip(values, -most, most).astype(dtype)


def gaussian_with(stream_key, dims, deviation, reach, pieces, heavy, dtype=jnp.bfloat16):
    values = deviation * jax.random.normal(stream_key, dims, jnp.float32)
    if pieces:
        values = values * level_of(stream_key, dims, pieces, -0.22, 0.18)
    return jnp.clip(strengthened(values, jax.random.fold_in(stream_key, 3), *heavy), -reach, reach).astype(dtype)


def setup_inputs(seed: int = 0, part: int = 0) -> dict:
    streams_of = jax.random.split(jax.random.key(seed), 7)
    part_splits = jax.random.split(jax.random.fold_in(streams_of[6], part), 7)
    return {
        "activations": gaussian_with(part_splits[0], (TOKENS, D), 1.0, 6.0, ((0, 8),), (0, 1, 8, 2.0)),
        "queries": noise(part_splits[1], (TOKENS, HEADS * HEAD_DIM), 1.0, 6.0, ((0, 8), (1, 2))),
        "key_rows": noise(part_splits[2], (TOKENS, HEADS * HEAD_DIM), 1.0, 6.0, ((0, 8), (1, 2))),
        "value_rows": noise(part_splits[3], (TOKENS, HEADS * HEAD_DIM), 1.0, 6.0, ((0, 8), (1, 2))),
        "out_grad": noise(part_splits[4], (TOKENS, HEADS * HEAD_DIM), 1.0, 6.0, ((0, 8), (1, 2))),
        "norm_gain": jnp.clip(1.0 + 0.18 * jax.random.normal(streams_of[5], (HEADS * HEAD_DIM,), jnp.float32), 0.1, 1.9),
    }


epsilon = 1e-06
highest = lax.Precision.HIGHEST

def split_state(state):
    high = state.astype(jnp.bfloat16)
    back = lax.optimization_barrier(high).astype(jnp.float32)
    low = (state - back).astype(jnp.bfloat16)
    return (high.astype(jnp.float32), low.astype(jnp.float32))

def masked_scores(left_side, right_side, causal):
    raw = jnp.einsum('thc,shc->hts', left_side.astype(jnp.float32), right_side.astype(jnp.float32), precision=highest)
    return jnp.where(causal[None], raw, 0.0).astype(jnp.bfloat16)

def norm_backward(attended, upstream_raw, gain_heads):
    inv_rms = lax.rsqrt(lax.optimization_barrier(jnp.mean(attended * attended, axis=-1, keepdims=True)) + epsilon)
    normed = attended * inv_rms
    upstream = upstream_raw.astype(jnp.float32) * gain_heads[None]
    delta = inv_rms * (upstream - normed * lax.optimization_barrier(jnp.mean(upstream * normed, axis=-1, keepdims=True)))
    return delta.astype(jnp.bfloat16)

def reference(activations, queries, key_rows, value_rows, out_grad, norm_gain):
    slabs = N_CTX
    length = TOK_DEV
    shape_four = (slabs, length, HEADS, HEAD_DIM)
    query_all = queries.reshape(shape_four)
    key_all = key_rows.reshape(shape_four)
    value_all = value_rows.reshape(shape_four)
    grad_all = out_grad.reshape(shape_four)
    gain_heads = norm_gain.reshape(HEADS, HEAD_DIM).astype(jnp.float32)
    causal = jnp.arange(length)[:, None] >= jnp.arange(length)[None, :]
    kv_local = jnp.einsum('nthc,nthd->nhcd', key_all.astype(jnp.float32), value_all.astype(jnp.float32), precision=highest)
    zero_state = jnp.zeros((1, HEADS, HEAD_DIM, HEAD_DIM), jnp.float32)
    state_in = jnp.concatenate([zero_state, jnp.cumsum(kv_local, axis=0)[:-1]], axis=0)

    def first_pass(items):
        query_slab, key_slab, value_slab, grad_slab, state_slab = items
        state_high, state_low = split_state(state_slab)
        query_wide = query_slab.astype(jnp.float32)
        scores = masked_scores(query_slab, key_slab, causal)
        attended = jnp.einsum('hts,shd->thd', scores.astype(jnp.float32), value_slab.astype(jnp.float32), precision=highest)
        attended = attended + jnp.einsum('thc,hcd->thd', query_wide, state_high, precision=highest)
        attended = attended + jnp.einsum('thc,hcd->thd', query_wide, state_low, precision=highest)
        delta = norm_backward(attended, grad_slab, gain_heads)
        grad_local = jnp.einsum('thc,thd->hcd', query_wide, delta.astype(jnp.float32), precision=highest)
        return (delta, grad_local)
    delta_all, grad_local = lax.map(first_pass, (query_all, key_all, value_all, grad_all, state_in))
    suffix = jnp.cumsum(grad_local[::-1], axis=0)[::-1]
    grad_in = jnp.concatenate([suffix[1:], zero_state], axis=0)

    def second_pass(items):
        query_slab, key_slab, value_slab, delta_slab, state_slab, grad_slab = items
        state_high, state_low = split_state(state_slab)
        grad_high, grad_low = split_state(grad_slab)
        scores = masked_scores(query_slab, key_slab, causal).astype(jnp.float32)
        back_scores = masked_scores(delta_slab, value_slab, causal).astype(jnp.float32)
        delta_wide = delta_slab.astype(jnp.float32)
        query_wide = query_slab.astype(jnp.float32)
        key_wide = key_slab.astype(jnp.float32)
        value_wide = value_slab.astype(jnp.float32)
        query_grad = jnp.einsum('hts,shc->thc', back_scores, key_wide, precision=highest)
        query_grad = query_grad + jnp.einsum('thd,hcd->thc', delta_wide, state_high, precision=highest)
        query_grad = query_grad + jnp.einsum('thd,hcd->thc', delta_wide, state_low, precision=highest)
        key_grad = jnp.einsum('hts,thc->shc', back_scores, query_wide, precision=highest)
        key_grad = key_grad + jnp.einsum('shd,hcd->shc', value_wide, grad_high, precision=highest)
        key_grad = key_grad + jnp.einsum('shd,hcd->shc', value_wide, grad_low, precision=highest)
        value_grad = jnp.einsum('hts,thd->shd', scores, delta_wide, precision=highest)
        value_grad = value_grad + jnp.einsum('shc,hcd->shd', key_wide, grad_high, precision=highest)
        value_grad = value_grad + jnp.einsum('shc,hcd->shd', key_wide, grad_low, precision=highest)
        return (query_grad.astype(jnp.bfloat16), key_grad.astype(jnp.bfloat16), value_grad.astype(jnp.bfloat16))
    query_grad, key_grad, value_grad = lax.map(second_pass, (query_all, key_all, value_all, delta_all, state_in, grad_in))
    value_slabs = value_grad.reshape(slabs, length, HEADS * HEAD_DIM)
    input_slabs = activations.reshape(slabs, length, D)

    def add_slab(running, items):
        input_slab, value_slab = items
        term = jnp.dot(input_slab.T, value_slab, preferred_element_type=jnp.float32)
        term = lax.optimization_barrier(term.astype(jnp.bfloat16)).astype(jnp.float32)
        return (running + term, None)
    weight_grad, unused = lax.scan(add_slab, jnp.zeros((D, HEADS * HEAD_DIM), jnp.float32), (input_slabs, value_slabs))
    flat_shape = (slabs * length, HEADS * HEAD_DIM)
    return (query_grad.reshape(flat_shape), key_grad.reshape(flat_shape), weight_grad)
```

```python
import functools

import jax
import jax.numpy as jnp
from jax import lax
from jax.experimental import pallas as pl
from jax.experimental.pallas import tpu as pltpu
from jax.sharding import PartitionSpec as P

HEAD_DIM = 128
EPSILON = 1e-06
MESH = pl.DeviceIdType.MESH
F32 = jnp.float32
BF16 = jnp.bfloat16


def dot(a, b, ca, cb):
    return lax.dot_general(a, b, (((ca,), (cb,)), ((), ())), preferred_element_type=F32)


def split_state(state):
    high = state.astype(BF16)
    return high, (state - high.astype(F32)).astype(BF16)


def kernel(
    n, chunks,
    act, q_in, k_in, v_in, g_in, gain,
    qg_out, kg_out, w_out,
    q, k, v, g, acts, vals, scores, delta, att, vg_acc, kg_acc, qg, kg, wg,
    kv_mine, kv_pair, kv_send, kv_recv, st_high, st_low,
    gl_mine, gl_pair, gl_send, gl_recv,
    right_out, right_in, left_out, left_in,
    in_sem, own_sem, out_sem,
    act_ssem, act_rsem, sib_sem,
    kvp_s, kvp_r, kvc_s, kvc_r,
    glp_s, glp_r, glc_s, glc_r,
    val_s, val_r,
    rt_s, rt_r, lt_s, lt_r,
):
    tok, width = q.shape
    heads = width // HEAD_DIM
    per = heads // chunks
    span = per * HEAD_DIM
    rows = n // 2
    own = act.shape[1] // n
    me = lax.axis_index("ctx")
    core = lax.axis_index("heads")
    z = me // 2
    y = me % 2
    pair = me + 1 - 2 * y
    half = rows // 2

    def load(i, src, dst):
        return pltpu.make_async_copy(src, dst, in_sem.at[i])

    loads = [load(0, k_in, k), load(1, v_in, v), load(2, q_in, q), load(3, g_in, g)]
    for c in loads:
        c.start()

    def own_act(b):
        src = pl.multiple_of((2 * b + y) * own, 128)
        return pltpu.make_async_copy(
            act.at[:, pl.ds(src, own)],
            acts.at[pl.ds(0, tok), pl.ds(pl.multiple_of(b * own, 128), own)],
            own_sem.at[b],
        )

    def send_act(j):
        b = core * half + j
        src = pl.multiple_of((2 * b + 1 - y) * own, 128)
        return pltpu.make_async_remote_copy(
            src_ref=act.at[:, pl.ds(src, own)],
            dst_ref=acts.at[pl.ds(tok, tok), pl.ds(pl.multiple_of(b * own, 128), own)],
            send_sem=act_ssem.at[j], recv_sem=act_rsem.at[j],
            device_id={"ctx": pair}, device_id_type=MESH,
        )

    def share_act():
        at = acts.at[pl.ds(tok, tok), pl.ds(pl.multiple_of(core * half * own, 128), half * own)]
        return pltpu.make_async_remote_copy(
            src_ref=at, dst_ref=at, send_sem=sib_sem.at[0], recv_sem=sib_sem.at[1],
            device_id={"heads": 1 - core}, device_id_type=MESH,
        )

    def heads_copy(src, dst, ssem, rsem, to, c):
        at = pl.ds(c * per, per)
        return pltpu.make_async_remote_copy(
            src_ref=src.at[at], dst_ref=dst.at[at],
            send_sem=ssem.at[c], recv_sem=rsem.at[c],
            device_id={"ctx": to}, device_id_type=MESH,
        )

    def send_val(c):
        cols = pl.ds(pl.multiple_of(c * span, 128), span)
        return pltpu.make_async_remote_copy(
            src_ref=vals.at[pl.ds(0, tok), cols], dst_ref=vals.at[pl.ds(tok, tok), cols],
            send_sem=val_s.at[c], recv_sem=val_r.at[c],
            device_id={"ctx": pair}, device_id_type=MESH,
        )

    def block_copy(src, dst, ssem, rsem, to, b, c):
        return pltpu.make_async_remote_copy(
            src_ref=src.at[b, c], dst_ref=dst.at[b, c],
            send_sem=ssem.at[b, c], recv_sem=rsem.at[b, c],
            device_id={"ctx": to}, device_id_type=MESH,
        )

    def right_copy(b, c):
        return block_copy(right_out, right_in, rt_s, rt_r, lax.rem(me + 2, n), b, c)

    def left_copy(b, c):
        return block_copy(left_out, left_in, lt_s, lt_r, lax.rem(me + n - 2, n), b, c)

    def kv_pair_copy(c):
        return heads_copy(kv_mine, kv_pair, kvp_s, kvp_r, pair, c)

    def kv_chain(c):
        return heads_copy(kv_send, kv_recv, kvc_s, kvc_r, lax.rem(me + 2, n), c)

    def gl_pair_copy(c):
        return heads_copy(gl_mine, gl_pair, glp_s, glp_r, pair, c)

    def gl_chain(c):
        return heads_copy(gl_send, gl_recv, glc_s, glc_r, lax.rem(me + n - 2, n), c)

    def loop(count, body):
        def step(i, carry):
            body(i)
            return carry
        lax.fori_loop(0, count, step, 0)

    def each_head(c, body):
        for i in range(per):
            h = c * per + i
            body(h, pl.ds(pl.multiple_of(h * HEAD_DIM, 128), HEAD_DIM))

    has_left = z > 0
    has_right = z < rows - 1

    barrier = pltpu.get_barrier_semaphore()
    pl.semaphore_signal(barrier, inc=1, device_id={"ctx": pair}, device_id_type=MESH)
    pl.semaphore_signal(barrier, inc=1, device_id={"heads": 1 - core}, device_id_type=MESH)

    @pl.when(has_left)
    def _():
        pl.semaphore_signal(barrier, inc=1, device_id={"ctx": me - 2}, device_id_type=MESH)

    @pl.when(has_right)
    def _():
        pl.semaphore_signal(barrier, inc=1, device_id={"ctx": me + 2}, device_id_type=MESH)

    ends = has_left.astype(jnp.int32) + has_right.astype(jnp.int32)
    pl.semaphore_wait(barrier, 2 + ends)

    loads[0].wait()
    loads[1].wait()

    def summaries(c):
        def one(h, cols):
            kv_mine[h] = dot(k[:, cols], v[:, cols], 0, 0).astype(BF16)
        each_head(c, one)
        kv_pair_copy(c).start()
    loop(chunks, summaries)

    loop(half, lambda j: send_act(j).start())
    loop(rows, lambda b: own_act(b).start())

    @pl.when(jnp.logical_not(has_left))
    def _():
        kv_recv[...] = jnp.zeros_like(kv_recv)

    @pl.when(jnp.logical_not(has_right))
    def _():
        gl_recv[...] = jnp.zeros_like(gl_recv)

    loads[2].wait()
    loads[3].wait()

    def causal(raw):
        t = lax.broadcasted_iota(jnp.int32, raw.shape, 0)
        s = lax.broadcasted_iota(jnp.int32, raw.shape, 1)
        return jnp.where(s <= t, raw, 0.0).astype(BF16)

    def score(c):
        def one(h, cols):
            s = causal(dot(q[:, cols], k[:, cols], 1, 1))
            scores[h] = s
            att[:, cols] = dot(s, v[:, cols], 1, 0)
        each_head(c, one)
    loop(chunks, score)

    def forward(c):
        kv_pair_copy(c).wait()

        @pl.when(has_left)
        def _():
            kv_chain(c).wait_recv()

        def state(h, cols):
            carry = kv_recv[h].astype(F32)
            other = kv_pair[h].astype(F32)
            kv_send[h] = (carry + other + kv_mine[h].astype(F32)).astype(BF16)
            high, low = split_state(carry + jnp.where(y == 1, other, 0.0))
            st_high[h] = high
            st_low[h] = low
        each_head(c, state)

        @pl.when(has_right)
        def _():
            kv_chain(c).start()

        def one(h, cols):
            qh = q[:, cols]
            a = att[:, cols] + dot(qh, st_high[h], 1, 0) + dot(qh, st_low[h], 1, 0)
            inv = lax.rsqrt(jnp.mean(a * a, axis=-1, keepdims=True) + EPSILON)
            normed = a * inv
            up = g[:, cols].astype(F32) * gain[:, cols]
            d = inv * (up - normed * jnp.mean(up * normed, axis=-1, keepdims=True))
            d = d.astype(BF16)
            delta[:, cols] = d
            gl_mine[h] = dot(qh, d, 0, 0).astype(BF16)
        each_head(c, one)
        gl_pair_copy(c).start()
    loop(chunks, forward)

    loop(half, lambda j: send_act(j).wait())
    share_act().start()

    def inside(c):
        def one(h, cols):
            d = delta[:, cols]
            back = causal(dot(d, v[:, cols], 1, 1))
            x = dot(back, k[:, cols], 1, 0)
            x = x + dot(d, st_high[h], 1, 1) + dot(d, st_low[h], 1, 1)
            qg[:, cols] = x.astype(BF16)
            kg_acc[:, cols] = dot(back, q[:, cols], 0, 0)
            vg_acc[:, cols] = dot(scores[h], d, 0, 0)
        each_head(c, one)
    loop(chunks, inside)
    qg_copy = pltpu.make_async_copy(qg, qg_out, out_sem.at[0])
    qg_copy.start()

    def backward(c):
        gl_pair_copy(c).wait()

        @pl.when(has_right)
        def _():
            gl_chain(c).wait_recv()

        def one(h, cols):
            carry = gl_recv[h].astype(F32)
            other = gl_pair[h].astype(F32)
            gl_send[h] = (carry + other + gl_mine[h].astype(F32)).astype(BF16)
        each_head(c, one)

        @pl.when(has_left)
        def _():
            gl_chain(c).start()

        def two(h, cols):
            carry = gl_recv[h].astype(F32)
            other = gl_pair[h].astype(F32)
            high, low = split_state(carry + jnp.where(y == 0, other, 0.0))
            kh = k[:, cols]
            x = vg_acc[:, cols] + dot(kh, high, 1, 0) + dot(kh, low, 1, 0)
            vals[0:tok, cols] = x.astype(BF16)
            vh = v[:, cols]
            x = kg_acc[:, cols] + dot(vh, high, 1, 1) + dot(vh, low, 1, 1)
            kg[:, cols] = x.astype(BF16)
        each_head(c, two)
        send_val(c).start()
    loop(chunks, backward)
    kg_copy = pltpu.make_async_copy(kg, kg_out, out_sem.at[1])
    kg_copy.start()

    loop(rows, lambda b: own_act(b).wait())
    share_act().wait()

    def term(b, c):
        a = acts[:, pl.ds(pl.multiple_of(b * own, 128), own)]
        x = vals[:, pl.ds(pl.multiple_of(c * span, 128), span)]
        return dot(a, x, 0, 0)

    def products(c):
        send_val(c).wait()

        def step(j):
            r = rows - 1 - j

            @pl.when(r > z)
            def _():
                x = term(r, c)

                @pl.when(has_left)
                def _():
                    right_copy(r, c).wait_recv()
                    right_out[r, c] = (x + right_in[r, c].astype(F32)).astype(BF16)

                @pl.when(jnp.logical_not(has_left))
                def _():
                    right_out[r, c] = x.astype(BF16)
                right_copy(r, c).start()

            @pl.when(j < z)
            def _():
                x = term(j, c)

                @pl.when(has_right)
                def _():
                    left_copy(j, c).wait_recv()
                    left_out[j, c] = (x + left_in[j, c].astype(F32)).astype(BF16)

                @pl.when(jnp.logical_not(has_right))
                def _():
                    left_out[j, c] = x.astype(BF16)
                left_copy(j, c).start()
        loop(rows, step)
        wg[c] = term(z, c)
    loop(chunks, products)

    def w_copy(c):
        return pltpu.make_async_copy(
            wg.at[c], w_out.at[:, pl.ds(pl.multiple_of(c * span, 128), span)], out_sem.at[2 + c]
        )

    def finish(c):
        @pl.when(has_left)
        def _():
            right_copy(z, c).wait_recv()
            wg[c] = wg[c] + right_in[z, c].astype(F32)

        @pl.when(has_right)
        def _():
            left_copy(z, c).wait_recv()
            wg[c] = wg[c] + left_in[z, c].astype(F32)
        w_copy(c).start()
    loop(chunks, finish)

    def drain(c):
        @pl.when(has_right)
        def _():
            kv_chain(c).wait_send()

        @pl.when(has_left)
        def _():
            gl_chain(c).wait_send()

        def step(b):
            @pl.when(b > z)
            def _():
                right_copy(b, c).wait_send()

            @pl.when(b < z)
            def _():
                left_copy(b, c).wait_send()
        loop(rows, step)
        w_copy(c).wait()
    loop(chunks, drain)
    qg_copy.wait()
    kg_copy.wait()


def per_device(n, activations, queries, key_rows, value_rows, out_grad, norm_gain):
    tok, width = queries.shape
    deep = activations.shape[1]
    own = deep // n
    rows = n // 2
    heads = width // HEAD_DIM
    chunks = 4
    span = width // chunks
    states = pltpu.VMEM((heads, HEAD_DIM, HEAD_DIM), BF16)
    blocks = pltpu.VMEM((rows, chunks, own, span), BF16)
    slab = pltpu.VMEM((tok, width), BF16)
    wide = pltpu.VMEM((tok, width), F32)
    dma = pltpu.SemaphoreType.DMA
    hbm = pl.BlockSpec(memory_space=pl.ANY)
    flops = 2 * tok * deep * width + 2 * heads * tok * HEAD_DIM * (6 * tok + 10 * HEAD_DIM)
    return pl.pallas_call(
        functools.partial(kernel, n, chunks),
        out_shape=(
            jax.ShapeDtypeStruct((tok, width), BF16),
            jax.ShapeDtypeStruct((tok, width), BF16),
            jax.ShapeDtypeStruct((own, width), F32),
        ),
        in_specs=[hbm] * 5 + [pl.BlockSpec(memory_space=pltpu.VMEM)],
        out_specs=(hbm, hbm, hbm),
        scratch_shapes=[
            slab, slab, slab, slab,
            pltpu.VMEM((2 * tok, rows * own), BF16),
            pltpu.VMEM((2 * tok, width), BF16),
            pltpu.VMEM((heads, tok, tok), BF16),
            slab, wide, wide, wide, slab, slab,
            pltpu.VMEM((chunks, own, span), F32),
        ] + [states] * 10 + [blocks] * 4 + [
            dma((4,)), dma((rows,)), dma((2 + chunks,)),
            dma((rows // 2,)), dma((rows // 2,)), dma((2,)),
        ] + [dma((chunks,))] * 10 + [dma((rows, chunks))] * 4,
        compiler_params=pltpu.CompilerParams(
            collective_id=0, has_side_effects=True, vmem_limit_bytes=60 * 1024 * 1024
        ),
        cost_estimate=pl.CostEstimate(flops=flops, bytes_accessed=17 * 2**20, transcendentals=0),
    )(activations, queries, key_rows, value_rows, out_grad, norm_gain.reshape(1, width))


def solution(mesh):
    rows = P(("groups", "ctx"), None)
    split = P(("groups", "ctx"), "heads")
    return jax.shard_map(
        functools.partial(per_device, mesh.shape["ctx"]),
        mesh=mesh,
        in_specs=(rows, split, split, split, split, P("heads")),
        out_specs=(split, split, split),
        check_vma=False,
    )
```

```python
import functools

import jax
import jax.numpy as jnp
from jax import lax
from jax.experimental import pallas as pl
from jax.experimental.pallas import tpu as pltpu
from jax.sharding import PartitionSpec as P

HEAD_DIM = 128
EPSILON = 1e-06
MESH = pl.DeviceIdType.MESH
F32 = jnp.float32
BF16 = jnp.bfloat16


def dot(a, b, ca, cb):
    return lax.dot_general(a, b, (((ca,), (cb,)), ((), ())), preferred_element_type=F32)


def split_state(state):
    high = state.astype(BF16)
    return high, (state - high.astype(F32)).astype(BF16)


def kernel(
    n, chunks,
    act, q_in, k_in, v_in, g_in, gain,
    qg_out, kg_out, w_out,
    q, k, v, g, acts, vals, scores, delta, att, vg_acc, kg_acc, qg, kg, wg,
    kv_mine, kv_pair, kv_send, kv_recv, st_high, st_low,
    gl_mine, gl_pair, gl_send, gl_recv,
    right_out, right_in, left_out, left_in, acts_edge, vals_edge,
    in_sem, own_sem, out_sem,
    act_ssem, act_rsem, sib_sem,
    kvp_s, kvp_r, kvc_s, kvc_r,
    glp_s, glp_r, glc_s, glc_r,
    val_s, val_r,
    rt_s, rt_r, lt_s, lt_r,
    ship_s, ship_r, relay_s, relay_r, vship_s, vship_r,
):
    tok, width = q.shape
    heads = width // HEAD_DIM
    per = heads // chunks
    span = per * HEAD_DIM
    rows = n // 2
    own = act.shape[1] // n
    me = lax.axis_index("ctx")
    core = lax.axis_index("heads")
    z = me // 2
    y = me % 2
    pair = me + 1 - 2 * y
    half = rows // 2
    near_left = z < half
    near_right = z >= half
    has_left = z > 0
    has_right = z < rows - 1
    middle = has_left & has_right
    edge = jnp.logical_not(middle)
    after_edge = z == 1
    before_edge = z == rows - 2
    inside_edge = after_edge | before_edge

    def load(i, src, dst):
        return pltpu.make_async_copy(src, dst, in_sem.at[i])

    loads = [load(0, k_in, k), load(1, v_in, v), load(2, q_in, q), load(3, g_in, g)]
    for c in loads:
        c.start()

    def own_act(b):
        src = pl.multiple_of((2 * b + y) * own, 128)
        return pltpu.make_async_copy(
            act.at[:, pl.ds(src, own)],
            acts.at[pl.ds(0, tok), pl.ds(pl.multiple_of(b * own, 128), own)],
            own_sem.at[b],
        )

    def send_act(j):
        b = core * half + j
        src = pl.multiple_of((2 * b + 1 - y) * own, 128)
        return pltpu.make_async_remote_copy(
            src_ref=act.at[:, pl.ds(src, own)],
            dst_ref=acts.at[pl.ds(tok, tok), pl.ds(pl.multiple_of(b * own, 128), own)],
            send_sem=act_ssem.at[j], recv_sem=act_rsem.at[j],
            device_id={"ctx": pair}, device_id_type=MESH,
        )

    def share_act():
        at = acts.at[pl.ds(tok, tok), pl.ds(pl.multiple_of(core * half * own, 128), half * own)]
        return pltpu.make_async_remote_copy(
            src_ref=at, dst_ref=at, send_sem=sib_sem.at[0], recv_sem=sib_sem.at[1],
            device_id={"heads": 1 - core}, device_id_type=MESH,
        )

    def edge_rows(p):
        return pl.ds(pl.multiple_of(p * tok + core * (tok // 2), 16), tok // 2)

    edge_cols = pl.ds(pl.multiple_of(jnp.where(near_left, own, 0), 128), (rows - 1) * own)
    inner = jnp.where(near_left, lax.rem(me + 2, n), lax.rem(me + n - 2, n))

    def ship(p):
        at = edge_rows(p)
        return pltpu.make_async_remote_copy(
            src_ref=acts.at[at, edge_cols], dst_ref=acts_edge.at[at, edge_cols],
            send_sem=ship_s.at[p], recv_sem=ship_r.at[p],
            device_id={"ctx": inner}, device_id_type=MESH,
        )

    def relay(p):
        at = acts_edge.at[edge_rows(p), edge_cols]
        return pltpu.make_async_remote_copy(
            src_ref=at, dst_ref=at, send_sem=relay_s.at[p], recv_sem=relay_r.at[p],
            device_id={"heads": 1 - core}, device_id_type=MESH,
        )

    def ship_val(p, c):
        at = pl.ds(p * tok, tok)
        cols = pl.ds(pl.multiple_of(c * span, 128), span)
        return pltpu.make_async_remote_copy(
            src_ref=vals.at[at, cols], dst_ref=vals_edge.at[at, cols],
            send_sem=vship_s.at[p, c], recv_sem=vship_r.at[p, c],
            device_id={"ctx": inner}, device_id_type=MESH,
        )

    def heads_copy(src, dst, ssem, rsem, to, c):
        at = pl.ds(c * per, per)
        return pltpu.make_async_remote_copy(
            src_ref=src.at[at], dst_ref=dst.at[at],
            send_sem=ssem.at[c], recv_sem=rsem.at[c],
            device_id={"ctx": to}, device_id_type=MESH,
        )

    def send_val(c):
        cols = pl.ds(pl.multiple_of(c * span, 128), span)
        return pltpu.make_async_remote_copy(
            src_ref=vals.at[pl.ds(0, tok), cols], dst_ref=vals.at[pl.ds(tok, tok), cols],
            send_sem=val_s.at[c], recv_sem=val_r.at[c],
            device_id={"ctx": pair}, device_id_type=MESH,
        )

    def block_copy(src, dst, ssem, rsem, to, b, c):
        return pltpu.make_async_remote_copy(
            src_ref=src.at[b, c], dst_ref=dst.at[b, c],
            send_sem=ssem.at[b, c], recv_sem=rsem.at[b, c],
            device_id={"ctx": to}, device_id_type=MESH,
        )

    def right_copy(b, c):
        return block_copy(right_out, right_in, rt_s, rt_r, lax.rem(me + 2, n), b, c)

    def left_copy(b, c):
        return block_copy(left_out, left_in, lt_s, lt_r, lax.rem(me + n - 2, n), b, c)

    def kv_pair_copy(c):
        return heads_copy(kv_mine, kv_pair, kvp_s, kvp_r, pair, c)

    def kv_chain(c):
        return heads_copy(kv_send, kv_recv, kvc_s, kvc_r, lax.rem(me + 2, n), c)

    def gl_pair_copy(c):
        return heads_copy(gl_mine, gl_pair, glp_s, glp_r, pair, c)

    def gl_chain(c):
        return heads_copy(gl_send, gl_recv, glc_s, glc_r, lax.rem(me + n - 2, n), c)

    def loop(count, body):
        def step(i, carry):
            body(i)
            return carry
        lax.fori_loop(0, count, step, 0)

    def each_head(c, body):
        for i in range(per):
            h = c * per + i
            body(h, pl.ds(pl.multiple_of(h * HEAD_DIM, 128), HEAD_DIM))

    barrier = pltpu.get_barrier_semaphore()
    pl.semaphore_signal(barrier, inc=1, device_id={"ctx": pair}, device_id_type=MESH)
    pl.semaphore_signal(barrier, inc=1, device_id={"heads": 1 - core}, device_id_type=MESH)

    @pl.when(has_left)
    def _():
        pl.semaphore_signal(barrier, inc=1, device_id={"ctx": me - 2}, device_id_type=MESH)

    @pl.when(has_right)
    def _():
        pl.semaphore_signal(barrier, inc=1, device_id={"ctx": me + 2}, device_id_type=MESH)

    ends = has_left.astype(jnp.int32) + has_right.astype(jnp.int32)
    pl.semaphore_wait(barrier, 2 + ends)

    @pl.when(near_right)
    def _():
        loop(half, lambda j: send_act(j).start())

    loop(rows, lambda b: own_act(b).start())
    loads[0].wait()
    loads[1].wait()

    def summaries(c):
        def one(h, cols):
            kv_mine[h] = dot(k[:, cols], v[:, cols], 0, 0).astype(BF16)
        each_head(c, one)
        kv_pair_copy(c).start()
    loop(chunks, summaries)

    loop(rows, lambda b: own_act(b).wait())

    @pl.when(jnp.logical_not(has_right))
    def _():
        ship(0).start()

    @pl.when(jnp.logical_not(has_left))
    def _():
        kv_recv[...] = jnp.zeros_like(kv_recv)

    @pl.when(jnp.logical_not(has_right))
    def _():
        gl_recv[...] = jnp.zeros_like(gl_recv)

    loads[2].wait()
    loads[3].wait()

    def causal(raw):
        t = lax.broadcasted_iota(jnp.int32, raw.shape, 0)
        s = lax.broadcasted_iota(jnp.int32, raw.shape, 1)
        return jnp.where(s <= t, raw, 0.0).astype(BF16)

    def score(c):
        def one(h, cols):
            s = causal(dot(q[:, cols], k[:, cols], 1, 1))
            scores[h] = s
            att[:, cols] = dot(s, v[:, cols], 1, 0)
        each_head(c, one)
    loop(chunks, score)

    def forward(c):
        kv_pair_copy(c).wait()

        @pl.when(near_left & (c == chunks - 1))
        def _():
            loop(half, lambda j: send_act(j).start())

        @pl.when(has_left)
        def _():
            kv_chain(c).wait_recv()

        def state(h, cols):
            carry = kv_recv[h].astype(F32)
            other = kv_pair[h].astype(F32)
            kv_send[h] = (carry + other + kv_mine[h].astype(F32)).astype(BF16)
            high, low = split_state(carry + jnp.where(y == 1, other, 0.0))
            st_high[h] = high
            st_low[h] = low
        each_head(c, state)

        @pl.when(has_right)
        def _():
            kv_chain(c).start()

        def one(h, cols):
            qh = q[:, cols]
            a = att[:, cols] + dot(qh, st_high[h], 1, 0) + dot(qh, st_low[h], 1, 0)
            inv = lax.rsqrt(jnp.mean(a * a, axis=-1, keepdims=True) + EPSILON)
            normed = a * inv
            up = g[:, cols].astype(F32) * gain[:, cols]
            d = inv * (up - normed * jnp.mean(up * normed, axis=-1, keepdims=True))
            d = d.astype(BF16)
            delta[:, cols] = d
            gl_mine[h] = dot(qh, d, 0, 0).astype(BF16)
        each_head(c, one)
        gl_pair_copy(c).start()
    loop(chunks, forward)

    def carry_grads(c):
        gl_pair_copy(c).wait()

        @pl.when(has_right)
        def _():
            gl_chain(c).wait_recv()

        def one(h, cols):
            carry = gl_recv[h].astype(F32)
            other = gl_pair[h].astype(F32)
            gl_send[h] = (carry + other + gl_mine[h].astype(F32)).astype(BF16)
        each_head(c, one)

        @pl.when(has_left)
        def _():
            gl_chain(c).start()

    def gather_act():
        loop(half, lambda j: send_act(j).wait())
        share_act().start()
        share_act().wait()

        @pl.when(edge)
        def _():
            ship(1).start()

    @pl.when(jnp.logical_not(has_left))
    def _():
        ship(0).start()

    @pl.when(jnp.logical_not(has_right))
    def _():
        loop(chunks, carry_grads)

    @pl.when(near_right)
    def _():
        gather_act()

    def inside(c):
        def one(h, cols):
            d = delta[:, cols]
            back = causal(dot(d, v[:, cols], 1, 1))
            x = dot(back, k[:, cols], 1, 0)
            x = x + dot(d, st_high[h], 1, 1) + dot(d, st_low[h], 1, 1)
            qg[:, cols] = x.astype(BF16)
            kg_acc[:, cols] = dot(back, q[:, cols], 0, 0)
            vg_acc[:, cols] = dot(scores[h], d, 0, 0)
        each_head(c, one)
    loop(chunks, inside)

    @pl.when(near_left)
    def _():
        gather_act()

    qg_copy = pltpu.make_async_copy(qg, qg_out, out_sem.at[0])
    qg_copy.start()

    def backward(c):
        @pl.when(has_right)
        def _():
            carry_grads(c)

        def two(h, cols):
            carry = gl_recv[h].astype(F32)
            other = gl_pair[h].astype(F32)
            high, low = split_state(carry + jnp.where(y == 0, other, 0.0))
            kh = k[:, cols]
            x = vg_acc[:, cols] + dot(kh, high, 1, 0) + dot(kh, low, 1, 0)
            vals[0:tok, cols] = x.astype(BF16)
            vh = v[:, cols]
            x = kg_acc[:, cols] + dot(vh, high, 1, 1) + dot(vh, low, 1, 1)
            kg[:, cols] = x.astype(BF16)
        each_head(c, two)
        send_val(c).start()

        @pl.when(edge)
        def _():
            ship_val(0, c).start()
    loop(chunks, backward)
    kg_copy = pltpu.make_async_copy(kg, kg_out, out_sem.at[1])
    kg_copy.start()

    @pl.when(inside_edge)
    def _():
        for p in range(2):
            ship(p).wait_recv()
            relay(p).start()
        for p in range(2):
            relay(p).wait()

    def term(b, c):
        a = acts[:, pl.ds(pl.multiple_of(b * own, 128), own)]
        x = vals[:, pl.ds(pl.multiple_of(c * span, 128), span)]
        return dot(a, x, 0, 0)

    def edge_term(b, c):
        a = acts_edge[:, pl.ds(pl.multiple_of(b * own, 128), own)]
        x = vals_edge[:, pl.ds(pl.multiple_of(c * span, 128), span)]
        return dot(a, x, 0, 0)

    def products(c):
        send_val(c).wait()

        @pl.when(edge)
        def _():
            ship_val(1, c).start()

        @pl.when(inside_edge)
        def _():
            ship_val(0, c).wait_recv()
            ship_val(1, c).wait_recv()

        def step(j):
            r = rows - 1 - j

            @pl.when(middle & (r > z))
            def _():
                x = term(r, c)

                @pl.when(after_edge)
                def _():
                    right_out[r, c] = (x + edge_term(r, c)).astype(BF16)

                @pl.when(jnp.logical_not(after_edge))
                def _():
                    right_copy(r, c).wait_recv()
                    right_out[r, c] = (x + right_in[r, c].astype(F32)).astype(BF16)
                right_copy(r, c).start()

            @pl.when(middle & (j < z))
            def _():
                x = term(j, c)

                @pl.when(before_edge)
                def _():
                    left_out[j, c] = (x + edge_term(j, c)).astype(BF16)

                @pl.when(jnp.logical_not(before_edge))
                def _():
                    left_copy(j, c).wait_recv()
                    left_out[j, c] = (x + left_in[j, c].astype(F32)).astype(BF16)
                left_copy(j, c).start()
        loop(rows, step)
        wg[c] = term(z, c)

        @pl.when(inside_edge)
        def _():
            wg[c] = wg[c] + edge_term(z, c)
    loop(chunks, products)

    def w_copy(c):
        return pltpu.make_async_copy(
            wg.at[c], w_out.at[:, pl.ds(pl.multiple_of(c * span, 128), span)], out_sem.at[2 + c]
        )

    def finish(c):
        @pl.when(z > 1)
        def _():
            right_copy(z, c).wait_recv()
            wg[c] = wg[c] + right_in[z, c].astype(F32)

        @pl.when(z < rows - 2)
        def _():
            left_copy(z, c).wait_recv()
            wg[c] = wg[c] + left_in[z, c].astype(F32)
        w_copy(c).start()
    loop(chunks, finish)

    def drain(c):
        @pl.when(has_right)
        def _():
            kv_chain(c).wait_send()

        @pl.when(has_left)
        def _():
            gl_chain(c).wait_send()

        def step(b):
            @pl.when(middle & (b > z))
            def _():
                right_copy(b, c).wait_send()

            @pl.when(middle & (b < z))
            def _():
                left_copy(b, c).wait_send()
        loop(rows, step)

        @pl.when(edge)
        def _():
            ship_val(0, c).wait_send()
            ship_val(1, c).wait_send()
        w_copy(c).wait()
    loop(chunks, drain)

    @pl.when(edge)
    def _():
        ship(0).wait_send()
        ship(1).wait_send()
    qg_copy.wait()
    kg_copy.wait()


def per_device(n, activations, queries, key_rows, value_rows, out_grad, norm_gain):
    tok, width = queries.shape
    deep = activations.shape[1]
    own = deep // n
    rows = n // 2
    heads = width // HEAD_DIM
    chunks = 4
    span = width // chunks
    states = pltpu.VMEM((heads, HEAD_DIM, HEAD_DIM), BF16)
    blocks = pltpu.VMEM((rows, chunks, own, span), BF16)
    slab = pltpu.VMEM((tok, width), BF16)
    wide = pltpu.VMEM((tok, width), F32)
    dma = pltpu.SemaphoreType.DMA
    hbm = pl.BlockSpec(memory_space=pl.ANY)
    flops = 2 * tok * deep * width + 2 * heads * tok * HEAD_DIM * (6 * tok + 10 * HEAD_DIM)
    return pl.pallas_call(
        functools.partial(kernel, n, chunks),
        out_shape=(
            jax.ShapeDtypeStruct((tok, width), BF16),
            jax.ShapeDtypeStruct((tok, width), BF16),
            jax.ShapeDtypeStruct((own, width), F32),
        ),
        in_specs=[hbm] * 5 + [pl.BlockSpec(memory_space=pltpu.VMEM)],
        out_specs=(hbm, hbm, hbm),
        scratch_shapes=[
            slab, slab, slab, slab,
            pltpu.VMEM((2 * tok, rows * own), BF16),
            pltpu.VMEM((2 * tok, width), BF16),
            pltpu.VMEM((heads, tok, tok), BF16),
            slab, wide, wide, wide, slab, slab,
            pltpu.VMEM((chunks, own, span), F32),
        ] + [states] * 10 + [blocks] * 4 + [
            pltpu.VMEM((2 * tok, rows * own), BF16), pltpu.VMEM((2 * tok, width), BF16),
            dma((4,)), dma((rows,)), dma((2 + chunks,)),
            dma((rows // 2,)), dma((rows // 2,)), dma((2,)),
        ] + [dma((chunks,))] * 10 + [dma((rows, chunks))] * 4 + [dma((2,))] * 4 + [dma((2, chunks))] * 2,
        compiler_params=pltpu.CompilerParams(
            collective_id=0, has_side_effects=True, vmem_limit_bytes=60 * 1024 * 1024
        ),
        cost_estimate=pl.CostEstimate(flops=flops, bytes_accessed=17 * 2**20, transcendentals=0),
    )(activations, queries, key_rows, value_rows, out_grad, norm_gain.reshape(1, width))


def solution(mesh):
    rows = P(("groups", "ctx"), None)
    split = P(("groups", "ctx"), "heads")
    return jax.shard_map(
        functools.partial(per_device, mesh.shape["ctx"]),
        mesh=mesh,
        in_specs=(rows, split, split, split, split, P("heads")),
        out_specs=(split, split, split),
        check_vma=False,
    )
```

```python
import functools

import jax
import jax.numpy as jnp
from jax import lax
from jax.experimental import pallas as pl
from jax.experimental.pallas import tpu as pltpu
from jax.sharding import PartitionSpec as P

HEAD_DIM = 128
EPSILON = 1e-06
MESH = pl.DeviceIdType.MESH
F32 = jnp.float32
BF16 = jnp.bfloat16


def dot(a, b, ca, cb):
    return lax.dot_general(a, b, (((ca,), (cb,)), ((), ())), preferred_element_type=F32)


def split_state(state):
    high = state.astype(BF16)
    return high, (state - high.astype(F32)).astype(BF16)


def kernel(
    n, chunks,
    act, q_in, k_in, v_in, g_in, gain,
    qg_out, kg_out, w_out,
    q, k, v, g, acts, vals, scores, delta, att, vg_acc, kg_acc, qg, kg, wg,
    kv_mine, kv_pair, kv_send, kv_recv, st_high, st_low,
    gl_mine, gl_pair, gl_send, gl_recv,
    right_out, right_in, left_out, left_in,
    in_sem, own_sem, out_sem,
    act_ssem, act_rsem, sib_sem,
    kvp_s, kvp_r, kvc_s, kvc_r,
    glp_s, glp_r, glc_s, glc_r,
    val_s, val_r,
    rt_s, rt_r, lt_s, lt_r,
):
    tok, width = q.shape
    heads = width // HEAD_DIM
    per = heads // chunks
    span = per * HEAD_DIM
    rows = n // 2
    own = act.shape[1] // n
    me = lax.axis_index("ctx")
    core = lax.axis_index("heads")
    z = me // 2
    y = me % 2
    pair = me + 1 - 2 * y
    half = rows // 2
    near_left = z < half
    near_right = z >= half

    def load(i, src, dst):
        return pltpu.make_async_copy(src, dst, in_sem.at[i])

    loads = [load(0, k_in, k), load(1, v_in, v), load(2, q_in, q), load(3, g_in, g)]
    for c in loads:
        c.start()

    def own_act(b):
        src = pl.multiple_of((2 * b + y) * own, 128)
        return pltpu.make_async_copy(
            act.at[:, pl.ds(src, own)],
            acts.at[pl.ds(0, tok), pl.ds(pl.multiple_of(b * own, 128), own)],
            own_sem.at[b],
        )

    def send_act(j):
        b = core * half + j
        src = pl.multiple_of((2 * b + 1 - y) * own, 128)
        return pltpu.make_async_remote_copy(
            src_ref=act.at[:, pl.ds(src, own)],
            dst_ref=acts.at[pl.ds(tok, tok), pl.ds(pl.multiple_of(b * own, 128), own)],
            send_sem=act_ssem.at[j], recv_sem=act_rsem.at[j],
            device_id={"ctx": pair}, device_id_type=MESH,
        )

    def share_act():
        at = acts.at[pl.ds(tok, tok), pl.ds(pl.multiple_of(core * half * own, 128), half * own)]
        return pltpu.make_async_remote_copy(
            src_ref=at, dst_ref=at, send_sem=sib_sem.at[0], recv_sem=sib_sem.at[1],
            device_id={"heads": 1 - core}, device_id_type=MESH,
        )

    def heads_copy(src, dst, ssem, rsem, to, c):
        at = pl.ds(c * per, per)
        return pltpu.make_async_remote_copy(
            src_ref=src.at[at], dst_ref=dst.at[at],
            send_sem=ssem.at[c], recv_sem=rsem.at[c],
            device_id={"ctx": to}, device_id_type=MESH,
        )

    def send_val(c):
        cols = pl.ds(pl.multiple_of(c * span, 128), span)
        return pltpu.make_async_remote_copy(
            src_ref=vals.at[pl.ds(0, tok), cols], dst_ref=vals.at[pl.ds(tok, tok), cols],
            send_sem=val_s.at[c], recv_sem=val_r.at[c],
            device_id={"ctx": pair}, device_id_type=MESH,
        )

    def block_copy(src, dst, ssem, rsem, to, b, c):
        return pltpu.make_async_remote_copy(
            src_ref=src.at[b, c], dst_ref=dst.at[b, c],
            send_sem=ssem.at[b, c], recv_sem=rsem.at[b, c],
            device_id={"ctx": to}, device_id_type=MESH,
        )

    def right_copy(b, c):
        return block_copy(right_out, right_in, rt_s, rt_r, lax.rem(me + 2, n), b, c)

    def left_copy(b, c):
        return block_copy(left_out, left_in, lt_s, lt_r, lax.rem(me + n - 2, n), b, c)

    def kv_pair_copy(c):
        return heads_copy(kv_mine, kv_pair, kvp_s, kvp_r, pair, c)

    def kv_chain(c):
        return heads_copy(kv_send, kv_recv, kvc_s, kvc_r, lax.rem(me + 2, n), c)

    def gl_pair_copy(c):
        return heads_copy(gl_mine, gl_pair, glp_s, glp_r, pair, c)

    def gl_chain(c):
        return heads_copy(gl_send, gl_recv, glc_s, glc_r, lax.rem(me + n - 2, n), c)

    def loop(count, body):
        def step(i, carry):
            body(i)
            return carry
        lax.fori_loop(0, count, step, 0)

    def each_head(c, body):
        for i in range(per):
            h = c * per + i
            body(h, pl.ds(pl.multiple_of(h * HEAD_DIM, 128), HEAD_DIM))

    has_left = z > 0
    has_right = z < rows - 1

    barrier = pltpu.get_barrier_semaphore()
    pl.semaphore_signal(barrier, inc=1, device_id={"ctx": pair}, device_id_type=MESH)
    pl.semaphore_signal(barrier, inc=1, device_id={"heads": 1 - core}, device_id_type=MESH)

    @pl.when(has_left)
    def _():
        pl.semaphore_signal(barrier, inc=1, device_id={"ctx": me - 2}, device_id_type=MESH)

    @pl.when(has_right)
    def _():
        pl.semaphore_signal(barrier, inc=1, device_id={"ctx": me + 2}, device_id_type=MESH)

    ends = has_left.astype(jnp.int32) + has_right.astype(jnp.int32)
    pl.semaphore_wait(barrier, 2 + ends)

    @pl.when(near_right)
    def _():
        loop(half, lambda j: send_act(j).start())

    loads[0].wait()
    loads[1].wait()

    def summaries(c):
        def one(h, cols):
            kv_mine[h] = dot(k[:, cols], v[:, cols], 0, 0).astype(BF16)
        each_head(c, one)
        kv_pair_copy(c).start()
    loop(chunks, summaries)

    loop(rows, lambda b: own_act(b).start())

    @pl.when(jnp.logical_not(has_left))
    def _():
        kv_recv[...] = jnp.zeros_like(kv_recv)

    @pl.when(jnp.logical_not(has_right))
    def _():
        gl_recv[...] = jnp.zeros_like(gl_recv)

    loads[2].wait()
    loads[3].wait()

    def causal(raw):
        t = lax.broadcasted_iota(jnp.int32, raw.shape, 0)
        s = lax.broadcasted_iota(jnp.int32, raw.shape, 1)
        return jnp.where(s <= t, raw, 0.0).astype(BF16)

    def score(c):
        def one(h, cols):
            s = causal(dot(q[:, cols], k[:, cols], 1, 1))
            scores[h] = s
            att[:, cols] = dot(s, v[:, cols], 1, 0)
        each_head(c, one)
    loop(chunks, score)

    def forward(c):
        kv_pair_copy(c).wait()

        @pl.when(near_left & (c == chunks - 1))
        def _():
            loop(half, lambda j: send_act(j).start())

        @pl.when(has_left)
        def _():
            kv_chain(c).wait_recv()

        def state(h, cols):
            carry = kv_recv[h].astype(F32)
            other = kv_pair[h].astype(F32)
            kv_send[h] = (carry + other + kv_mine[h].astype(F32)).astype(BF16)
            high, low = split_state(carry + jnp.where(y == 1, other, 0.0))
            st_high[h] = high
            st_low[h] = low
        each_head(c, state)

        @pl.when(has_right)
        def _():
            kv_chain(c).start()

        def one(h, cols):
            qh = q[:, cols]
            a = att[:, cols] + dot(qh, st_high[h], 1, 0) + dot(qh, st_low[h], 1, 0)
            inv = lax.rsqrt(jnp.mean(a * a, axis=-1, keepdims=True) + EPSILON)
            normed = a * inv
            up = g[:, cols].astype(F32) * gain[:, cols]
            d = inv * (up - normed * jnp.mean(up * normed, axis=-1, keepdims=True))
            d = d.astype(BF16)
            delta[:, cols] = d
            gl_mine[h] = dot(qh, d, 0, 0).astype(BF16)
        each_head(c, one)
        gl_pair_copy(c).start()
    loop(chunks, forward)

    def carry_grads(c):
        gl_pair_copy(c).wait()

        @pl.when(has_right)
        def _():
            gl_chain(c).wait_recv()

        def one(h, cols):
            carry = gl_recv[h].astype(F32)
            other = gl_pair[h].astype(F32)
            gl_send[h] = (carry + other + gl_mine[h].astype(F32)).astype(BF16)
        each_head(c, one)

        @pl.when(has_left)
        def _():
            gl_chain(c).start()

    @pl.when(jnp.logical_not(has_right))
    def _():
        loop(chunks, carry_grads)

    def inside(c):
        def one(h, cols):
            d = delta[:, cols]
            back = causal(dot(d, v[:, cols], 1, 1))
            x = dot(back, k[:, cols], 1, 0)
            x = x + dot(d, st_high[h], 1, 1) + dot(d, st_low[h], 1, 1)
            qg[:, cols] = x.astype(BF16)
            kg_acc[:, cols] = dot(back, q[:, cols], 0, 0)
            vg_acc[:, cols] = dot(scores[h], d, 0, 0)
        each_head(c, one)
    loop(chunks, inside)
    qg_copy = pltpu.make_async_copy(qg, qg_out, out_sem.at[0])
    qg_copy.start()

    def backward(c):
        @pl.when(has_right)
        def _():
            carry_grads(c)

        def two(h, cols):
            carry = gl_recv[h].astype(F32)
            other = gl_pair[h].astype(F32)
            high, low = split_state(carry + jnp.where(y == 0, other, 0.0))
            kh = k[:, cols]
            x = vg_acc[:, cols] + dot(kh, high, 1, 0) + dot(kh, low, 1, 0)
            vals[0:tok, cols] = x.astype(BF16)
            vh = v[:, cols]
            x = kg_acc[:, cols] + dot(vh, high, 1, 1) + dot(vh, low, 1, 1)
            kg[:, cols] = x.astype(BF16)
        each_head(c, two)
        send_val(c).start()
    loop(chunks, backward)
    kg_copy = pltpu.make_async_copy(kg, kg_out, out_sem.at[1])
    kg_copy.start()

    loop(rows, lambda b: own_act(b).wait())
    loop(half, lambda j: send_act(j).wait())
    share_act().start()
    share_act().wait()

    def term(b, c):
        a = acts[:, pl.ds(pl.multiple_of(b * own, 128), own)]
        x = vals[:, pl.ds(pl.multiple_of(c * span, 128), span)]
        return dot(a, x, 0, 0)

    def products(c):
        send_val(c).wait()

        def step(j):
            r = rows - 1 - j

            @pl.when(r > z)
            def _():
                x = term(r, c)

                @pl.when(has_left)
                def _():
                    right_copy(r, c).wait_recv()
                    right_out[r, c] = (x + right_in[r, c].astype(F32)).astype(BF16)

                @pl.when(jnp.logical_not(has_left))
                def _():
                    right_out[r, c] = x.astype(BF16)
                right_copy(r, c).start()

            @pl.when(j < z)
            def _():
                x = term(j, c)

                @pl.when(has_right)
                def _():
                    left_copy(j, c).wait_recv()
                    left_out[j, c] = (x + left_in[j, c].astype(F32)).astype(BF16)

                @pl.when(jnp.logical_not(has_right))
                def _():
                    left_out[j, c] = x.astype(BF16)
                left_copy(j, c).start()
        loop(rows, step)
        wg[c] = term(z, c)
    loop(chunks, products)

    def w_copy(c):
        return pltpu.make_async_copy(
            wg.at[c], w_out.at[:, pl.ds(pl.multiple_of(c * span, 128), span)], out_sem.at[2 + c]
        )

    def finish(c):
        @pl.when(has_left)
        def _():
            right_copy(z, c).wait_recv()
            wg[c] = wg[c] + right_in[z, c].astype(F32)

        @pl.when(has_right)
        def _():
            left_copy(z, c).wait_recv()
            wg[c] = wg[c] + left_in[z, c].astype(F32)
        w_copy(c).start()
    loop(chunks, finish)

    def drain(c):
        @pl.when(has_right)
        def _():
            kv_chain(c).wait_send()

        @pl.when(has_left)
        def _():
            gl_chain(c).wait_send()

        def step(b):
            @pl.when(b > z)
            def _():
                right_copy(b, c).wait_send()

            @pl.when(b < z)
            def _():
                left_copy(b, c).wait_send()
        loop(rows, step)
        w_copy(c).wait()
    loop(chunks, drain)
    qg_copy.wait()
    kg_copy.wait()


def per_device(n, activations, queries, key_rows, value_rows, out_grad, norm_gain):
    tok, width = queries.shape
    deep = activations.shape[1]
    own = deep // n
    rows = n // 2
    heads = width // HEAD_DIM
    chunks = 4
    span = width // chunks
    states = pltpu.VMEM((heads, HEAD_DIM, HEAD_DIM), BF16)
    blocks = pltpu.VMEM((rows, chunks, own, span), BF16)
    slab = pltpu.VMEM((tok, width), BF16)
    wide = pltpu.VMEM((tok, width), F32)
    dma = pltpu.SemaphoreType.DMA
    hbm = pl.BlockSpec(memory_space=pl.ANY)
    flops = 2 * tok * deep * width + 2 * heads * tok * HEAD_DIM * (6 * tok + 10 * HEAD_DIM)
    return pl.pallas_call(
        functools.partial(kernel, n, chunks),
        out_shape=(
            jax.ShapeDtypeStruct((tok, width), BF16),
            jax.ShapeDtypeStruct((tok, width), BF16),
            jax.ShapeDtypeStruct((own, width), F32),
        ),
        in_specs=[hbm] * 5 + [pl.BlockSpec(memory_space=pltpu.VMEM)],
        out_specs=(hbm, hbm, hbm),
        scratch_shapes=[
            slab, slab, slab, slab,
            pltpu.VMEM((2 * tok, rows * own), BF16),
            pltpu.VMEM((2 * tok, width), BF16),
            pltpu.VMEM((heads, tok, tok), BF16),
            slab, wide, wide, wide, slab, slab,
            pltpu.VMEM((chunks, own, span), F32),
        ] + [states] * 10 + [blocks] * 4 + [
            dma((4,)), dma((rows,)), dma((2 + chunks,)),
            dma((rows // 2,)), dma((rows // 2,)), dma((2,)),
        ] + [dma((chunks,))] * 10 + [dma((rows, chunks))] * 4,
        compiler_params=pltpu.CompilerParams(
            collective_id=0, has_side_effects=True, vmem_limit_bytes=60 * 1024 * 1024
        ),
        cost_estimate=pl.CostEstimate(flops=flops, bytes_accessed=17 * 2**20, transcendentals=0),
    )(activations, queries, key_rows, value_rows, out_grad, norm_gain.reshape(1, width))


def solution(mesh):
    rows = P(("groups", "ctx"), None)
    split = P(("groups", "ctx"), "heads")
    return jax.shard_map(
        functools.partial(per_device, mesh.shape["ctx"]),
        mesh=mesh,
        in_specs=(rows, split, split, split, split, P("heads")),
        out_specs=(split, split, split),
        check_vma=False,
    )
```
